32 devices in a mesh: order: 8 (over y, x, core), chan: 4 (over z).
Axes of the slice: x: 2, y: 2, z: 4, core: 2. Of those that a mesh axis runs over, the one named last changes fastest.
Arguments:
- fields: bfloat16 [32, 3, 720, 2, 2, 256], P('order', None, None, None, None, 'chan'), may hold values from -6 to 6
- wigner: bfloat16 [32, 3, 721, 720], P('order'), may hold values from -0.21875 to 0.21875
- mix_weight: bfloat16 [736, 3, 256, 256], P('order', None, 'chan'), may hold values from -0.375 to 0.375
- pair_orders: int32 [32], P('order'), may hold values from 0 to 359, as said below
- deg_counts: int32 [8], replicated, may hold values from 1 to 92, 720 in all
Outputs:
- out_fields: bfloat16 [32, 3, 720, 2, 2, 256], P('order', None, None, None, None, 'chan')
The draws below stay inside these ranges and needn't reach their ends.
Inputs may be any that keep to these rules, and one draw needn't show every extreme that they name: Distinct lower orders; pair i holds orders m = pair_orders[i] and 719 - m, and pair i lies on order device i // 4. Owner e holds the next deg_counts[e] degrees after those of owners before it, in slots e * 92 onward, one slot each; the counts sum to 720, and slots past an owner's count are not read.
All inputs are finite; a program needn't handle non-finite values.
Results may differ from the reference program's by a relative error of at most 0.012.
Values may be sent and summed in bfloat16 or wider, within the bound.
A program may use at most 256 MiB of HBM per device.

```python
import math
import jax
import jax.numpy as jnp
import numpy as np
from jax import lax

L = 720
C = 256
CYCLES = 720
SPINS = 3
PAIRS = 32
OWNERS = 8
CHAN_BLOCKS = 4
DEG_SLOTS = 92
SLOT_ROWS = 736


def draw_pair_orders(key, part):
    key = jax.random.fold_in(key, 17)
    first_key, second_key = jax.random.split(key)
    band_end = L // 2
    middle_orders = jax.random.permutation(first_key, jnp.arange(1, band_end - 1, dtype=jnp.int32))[:PAIRS - 2]
    chosen_orders = jnp.concatenate([jnp.array([0, band_end - 1], dtype=jnp.int32), middle_orders])
    return jax.random.permutation(second_key, chosen_orders).astype(jnp.int32)


def levels(own_key, extent, pieces, smallest, high):
    factor_of, own = 1.0, jax.random.fold_in(own_key, 6)
    for axis_at, blocks in pieces:
        heights = jnp.exp(jax.random.uniform(jax.random.fold_in(own, axis_at), (blocks,), jnp.float32, smallest / len(pieces), high / len(pieces)))
        factor_of = factor_of * jnp.repeat(heights, extent[axis_at] // blocks).reshape([-1 if axis == axis_at else 1 for axis in range(len(extent))])
    return factor_of


def split_up(number_of, total, bound, slope):
    loads = [(1 << 20) // math.isqrt(standing ** slope) + 1 for standing in range(2, number_of + 1)]
    surplus, given = total - bound - (number_of - 1), [1] * (number_of - 1)
    while surplus > 0:
        candidates = [i for i in range(number_of - 1) if given[i] < bound]
        whole, budget = sum([loads[i] for i in candidates]), surplus
        for i in candidates:
            more = min(bound - given[i], max(1, budget * loads[i] // whole), surplus)
            given[i] = given[i] + more
            surplus = surplus - more
    return np.array([bound] + given)


def ragged_sizes(stream_key, number_of, total, reach, skew):
    if number_of == 2:
        one = jax.random.randint(stream_key, (), max(1, total - reach), min(reach, total - 1) + 1)
        return jnp.stack([one, total - one])
    lengths = jnp.asarray(split_up(number_of, total, reach, skew), jnp.int32)
    pairs = (number_of - 1) // 2
    giver, sink = lengths[1:1 + 2 * pairs:2], lengths[2:2 + 2 * pairs:2]
    margin = jnp.minimum(giver - 1, reach - sink)
    moved = jax.random.randint(jax.random.fold_in(stream_key, 1), (pairs,), 0, 1 << 20) % (margin + 1)
    lengths = lengths.at[1:1 + 2 * pairs:2].set(giver - moved).at[2:2 + 2 * pairs:2].set(sink + moved)
    return lengths[jax.random.permutation(jax.random.fold_in(stream_key, 2), number_of)]


def centred(rng, dims, deviation, reach, cuts=(), held_as=jnp.bfloat16):
    drawn = jax.random.normal(rng, dims, jnp.float32) * deviation
    if len(cuts) > 0:
        drawn = levels(rng, dims, cuts, -0.22, 0.18) * drawn
    return jnp.clip(drawn, min=-reach, max=reach).astype(held_as)


def setup_inputs(seed: int = 0) -> dict:
    arg_keys = jax.random.split(jax.random.key(seed), 6)
    fields = centred(arg_keys[0], (PAIRS, SPINS, CYCLES, 2, 2, C), 1.0, 6.0, ((0, 8), (5, 4)))
    wigner = centred(arg_keys[1], (PAIRS, SPINS, L + 1, CYCLES), CYCLES ** -0.5, 0.21875, ((0, 8),))
    mix_weight = centred(arg_keys[2], (SLOT_ROWS, SPINS, C, C), C ** -0.5, 0.375, ((0, 8), (2, 4)))
    pair_orders = draw_pair_orders(jax.random.fold_in(arg_keys[5], 71), 0)
    deg_counts = ragged_sizes(arg_keys[4], OWNERS, L, DEG_SLOTS, 0).astype(jnp.int32)
    return dict(fields=fields, wigner=wigner, mix_weight=mix_weight, pair_orders=pair_orders, deg_counts=deg_counts)


def slot_for(degree, ends_at, slot_count):
    above = (degree[..., None] >= ends_at).astype(jnp.int32)
    owner_of = jnp.sum(above, axis=-1).astype(jnp.int32)
    start_of = jnp.max(jnp.where(above > 0, ends_at, 0), axis=-1).astype(jnp.int32)
    return (owner_of * slot_count + degree - start_of).astype(jnp.int32)


def reference(fields, wigner, mix_weight, pair_orders, deg_counts):
    ends_at = jnp.cumsum(deg_counts).astype(jnp.int32)
    degree_iota = jnp.arange(L, dtype=jnp.int32)
    row_iota = jnp.arange(L + 1, dtype=jnp.int32)
    weight_rows = mix_weight[slot_for(degree_iota, ends_at, DEG_SLOTS)].astype(jnp.float32)
    weight_blocks = weight_rows.reshape(L, SPINS, CHAN_BLOCKS, C // CHAN_BLOCKS, C)

    def one_pair(entry):
        table_rows, field_rows, low_order = entry
        table_rows = table_rows.astype(jnp.float32)
        field_rows = field_rows.astype(jnp.float32)
        high_order = L - 1 - low_order
        coefficients = jnp.einsum("srj,sjoxc->sorxc", table_rows, field_rows).astype(jnp.bfloat16)
        lower_index = jnp.clip(degree_iota - low_order, 0, L).astype(jnp.int32)
        lower_coef = jnp.take(coefficients[:, 0], lower_index, axis=1)
        lower_coef = jnp.where((degree_iota >= low_order)[None, :, None, None], lower_coef, jnp.zeros_like(lower_coef))
        higher_coef = jnp.take(coefficients[:, 1], (degree_iota + 1).astype(jnp.int32), axis=1)
        higher_coef = jnp.where((degree_iota >= high_order)[None, :, None, None], higher_coef, jnp.zeros_like(higher_coef))
        both_orders = jnp.stack([lower_coef, higher_coef], axis=1).astype(jnp.float32)
        blocked = both_orders.reshape(SPINS, 2, L, 2, CHAN_BLOCKS, C // CHAN_BLOCKS)
        partials = jnp.einsum("solxgc,lsgcd->solxgd", blocked, weight_blocks).astype(jnp.bfloat16)
        partials = lax.optimization_barrier(partials)
        mixed_coef = jnp.sum(partials.astype(jnp.float32), axis=4).astype(jnp.bfloat16)
        lower_degree = (low_order + row_iota).astype(jnp.int32)
        lower_back = jnp.take(mixed_coef[:, 0], jnp.clip(lower_degree, 0, L - 1), axis=1)
        lower_back = jnp.where((lower_degree < L)[None, :, None, None], lower_back, jnp.zeros_like(lower_back))
        higher_degree = (row_iota - 1).astype(jnp.int32)
        higher_back = jnp.take(mixed_coef[:, 1], jnp.clip(higher_degree, 0, L - 1), axis=1)
        higher_back = jnp.where((higher_degree >= high_order)[None, :, None, None], higher_back, jnp.zeros_like(higher_back))
        lower_field = jnp.einsum("srj,srxd->sjxd", table_rows, lower_back.astype(jnp.float32))
        higher_field = jnp.einsum("srj,srxd->sjxd", table_rows, higher_back.astype(jnp.float32))
        return jnp.stack([lower_field, higher_field], axis=2).astype(jnp.bfloat16)

    return lax.map(one_pair, (wigner, fields, pair_orders))
```

```python
import functools
import jax
import jax.numpy as jnp
from jax import lax
from jax.experimental import pallas as pl
from jax.experimental.pallas import tpu as pltpu
from jax.sharding import PartitionSpec as P

F32, BF16 = jnp.float32, jnp.bfloat16
FIRST = (((0,), (0,)), ((), ()))
LAST = (((1,), (1,)), ((), ()))
PARAMS = pltpu.CompilerParams(vmem_limit_bytes=48 * 1024 * 1024)


def analyse_kernel(order_ref, degree_ref, table_ref, field_ref, out_ref, low_pick, high_pick):
    pair = pl.program_id(0)
    rows = table_ref.shape[3]
    half = field_ref.shape[2] // 2

    @pl.when(pl.program_id(1) == 0)
    def _():
        low = order_ref[pair]
        degree = degree_ref[...]
        at = lax.broadcasted_iota(jnp.int32, low_pick.shape, 1)
        low_pick[...] = jnp.where(at == degree - low, 1.0, 0.0).astype(BF16)
        high = jnp.where(degree >= rows - 2 - low, degree + 1, -1)
        high_pick[...] = jnp.where(at == high, 1.0, 0.0).astype(BF16)

    coef = jnp.dot(field_ref[0, 0], table_ref[0, 0], preferred_element_type=F32).astype(BF16)
    low_rows = lax.dot_general(low_pick[...], coef[:half], LAST, preferred_element_type=F32)
    high_rows = lax.dot_general(high_pick[...], coef[half:], LAST, preferred_element_type=F32)
    dests, _, _, slots, _ = out_ref.shape
    out_ref[:, 0, 0, :, :half] = low_rows.reshape(dests, slots, half).astype(BF16)
    out_ref[:, 0, 0, :, half:] = high_rows.reshape(dests, slots, half).astype(BF16)


def synthesise_kernel(order_ref, degree_ref, table_ref, mixed_ref, out_ref, low_pick, high_pick):
    pair = pl.program_id(0)
    rows = table_ref.shape[3]
    half = mixed_ref.shape[4] // 2

    @pl.when(pl.program_id(1) == 0)
    def _():
        low = order_ref[pair]
        degree = degree_ref[...]
        at = lax.broadcasted_iota(jnp.int32, low_pick.shape, 1)
        low_pick[...] = jnp.where(at == degree - low, 1.0, 0.0).astype(BF16)
        high = jnp.where(degree >= rows - 2 - low, degree + 1, -1)
        high_pick[...] = jnp.where(at == high, 1.0, 0.0).astype(BF16)

    dests, _, _, slots, width = mixed_ref.shape
    mixed = mixed_ref[:, 0, 0].astype(F32).reshape(dests * slots, width).astype(BF16)
    low_rows = lax.dot_general(mixed[:, :half], low_pick[...], FIRST, preferred_element_type=F32)
    high_rows = lax.dot_general(mixed[:, half:], high_pick[...], FIRST, preferred_element_type=F32)
    back = jnp.concatenate([low_rows, high_rows], axis=0).astype(BF16)
    out_ref[0, 0] = lax.dot_general(
        back, table_ref[0, 0], LAST, preferred_element_type=F32
    ).astype(BF16)


def mix_kernel(slot_count, where_ref, x_ref, *refs):
    weights, out_ref = refs[:-1], refs[-1]
    blocks = len(weights)
    _, spins, _, items, width = x_ref.shape
    chans = weights[0].shape[2]
    parts = width // chans
    me = where_ref[0]
    live = pl.program_id(0) < slot_count

    @pl.when(live)
    def _():
        for s in range(spins):
            held = []
            for shift in range(blocks):
                x = x_ref[0, s, lax.rem(me - shift + blocks, blocks)]
                held.append(
                    jnp.concatenate([x[:, i * chans:(i + 1) * chans] for i in range(parts)], axis=0)
                )
            w = jnp.concatenate([weight[0, s] for weight in weights], axis=0)
            y = jnp.dot(jnp.concatenate(held, axis=1), w, preferred_element_type=F32).astype(BF16)
            for g in range(blocks):
                out_ref[0, s, g] = jnp.concatenate(
                    [y[i * items:(i + 1) * items, g * chans:(g + 1) * chans] for i in range(parts)],
                    axis=1,
                )

    @pl.when(jnp.logical_not(live))
    def _():
        out_ref[...] = jnp.zeros_like(out_ref)


def per_device(fields, wigner, mix_weight, pair_orders, deg_counts):
    pairs, spins, cycles, _, _, chans = fields.shape
    rows = wigner.shape[2]
    width = 4 * chans
    owners, blocks = lax.axis_size("order"), lax.axis_size("chan")
    slots = mix_weight.shape[0] // blocks
    padded = -(-slots // 8) * 8
    dests = owners * blocks
    me = lax.axis_index("chan")

    starts = jnp.cumsum(deg_counts) - deg_counts
    within = jnp.arange(padded, dtype=jnp.int32)
    slot = jnp.arange(blocks, dtype=jnp.int32)[:, None] * slots + within[None, :]
    real = (within[None, None, :] < slots) & (slot[None] < deg_counts[:, None, None])
    degree = jnp.where(real, starts[:, None, None] + slot[None], -(1 << 20)).reshape(-1, 1)
    total = dests * padded

    sent = []
    for shift in range(1, blocks):
        to = lax.rem(me + shift, blocks)
        sent.append(lax.dynamic_slice_in_dim(mix_weight, to * slots, slots, axis=0))
    degree, *sent = lax.optimization_barrier((degree, *sent))
    weights = [mix_weight]
    for shift in range(1, blocks):
        ring = [(g, (g + shift) % blocks) for g in range(blocks)]
        weights.append(lax.ppermute(sent[shift - 1], "chan", ring))
    table = wigner.transpose(0, 1, 3, 2)
    lines = fields.transpose(0, 1, 3, 4, 5, 2).reshape(pairs, spins, width, cycles)

    table_spec = pl.BlockSpec((1, 1, cycles, rows), lambda p, s, o: (p, s, 0, 0))
    field_spec = pl.BlockSpec((1, 1, width, cycles), lambda p, s, o: (p, s, 0, 0))
    moved_spec = pl.BlockSpec((dests, 1, 1, padded, width), lambda p, s, o: (0, p, s, 0, 0))
    moved = jax.ShapeDtypeStruct((dests, pairs, spins, padded, width), BF16)
    table_flops = 4 * pairs * spins * rows * cycles * width
    cost = pl.CostEstimate(flops=table_flops, bytes_accessed=2 * wigner.size * 2, transcendentals=0)

    outgoing = pl.pallas_call(
        analyse_kernel,
        out_shape=moved,
        grid_spec=pltpu.PrefetchScalarGridSpec(
            num_scalar_prefetch=1,
            grid=(pairs, spins),
            in_specs=[pl.BlockSpec((total, 1), lambda p, s, o: (0, 0)), table_spec, field_spec],
            out_specs=moved_spec,
            scratch_shapes=[pltpu.VMEM((total, rows), BF16)] * 2,
        ),
        compiler_params=PARAMS,
        cost_estimate=cost,
        name="analyse",
    )(pair_orders, degree, table, lines)

    received = lax.all_to_all(outgoing, ("order", "chan"), split_axis=0, concat_axis=0, tiled=True)
    received = received.reshape(owners, blocks, pairs, spins, padded, width)
    items = owners * pairs
    x = received.transpose(4, 3, 1, 0, 2, 5).reshape(padded, spins, blocks, items, width)

    def block_at(k):
        return jnp.minimum(k, slots - 1)

    weight_block = (1, spins, chans, mix_weight.shape[3])
    weight_specs = [pl.BlockSpec(weight_block, lambda k, w: (w[0] * slots + block_at(k), 0, 0, 0))]
    weight_specs += [pl.BlockSpec(weight_block, lambda k, w: (block_at(k), 0, 0, 0))] * (blocks - 1)
    x_spec = pl.BlockSpec((1, spins, blocks, items, width), lambda k, w: (k, 0, 0, 0, 0))
    mixed = pl.pallas_call(
        functools.partial(mix_kernel, slots),
        out_shape=jax.ShapeDtypeStruct(x.shape, BF16),
        grid_spec=pltpu.PrefetchScalarGridSpec(
            num_scalar_prefetch=1,
            grid=(padded,),
            in_specs=[x_spec] + weight_specs,
            out_specs=x_spec,
        ),
        compiler_params=PARAMS,
        name="mix",
    )(me.reshape(1).astype(jnp.int32), x, *weights)

    mixed = mixed.reshape(padded, spins, blocks, owners, pairs, width).transpose(3, 2, 4, 1, 0, 5)
    mixed = mixed.reshape(dests, pairs, spins, padded, width)
    returned = lax.all_to_all(mixed, ("order", "chan"), split_axis=0, concat_axis=0, tiled=True)

    out = pl.pallas_call(
        synthesise_kernel,
        out_shape=jax.ShapeDtypeStruct((pairs, spins, width, cycles), BF16),
        grid_spec=pltpu.PrefetchScalarGridSpec(
            num_scalar_prefetch=1,
            grid=(pairs, spins),
            in_specs=[pl.BlockSpec((total, 1), lambda p, s, o: (0, 0)), table_spec, moved_spec],
            out_specs=field_spec,
            scratch_shapes=[pltpu.VMEM((total, rows), BF16)] * 2,
        ),
        compiler_params=PARAMS,
        cost_estimate=cost,
        name="synthesise",
    )(pair_orders, degree, table, returned)
    return out.reshape(pairs, spins, 2, 2, chans, cycles).transpose(0, 1, 5, 2, 3, 4)


def solution(mesh):
    in_specs = (
        P("order", None, None, None, None, "chan"),
        P("order", None, None, None),
        P("order", None, "chan", None),
        P("order"),
        P(),
    )
    out_specs = P("order", None, None, None, None, "chan")
    return jax.shard_map(
        per_device, mesh=mesh, in_specs=in_specs, out_specs=out_specs, check_vma=False
    )
```

```python
import functools
import jax
import jax.numpy as jnp
from jax import lax
from jax.experimental import pallas as pl
from jax.experimental.pallas import tpu as pltpu
from jax.sharding import PartitionSpec as P

F32, BF16 = jnp.float32, jnp.bfloat16
FIRST = (((0,), (0,)), ((), ()))
LAST = (((1,), (1,)), ((), ()))
PARAMS = pltpu.CompilerParams(vmem_limit_bytes=48 * 1024 * 1024)


def analyse_kernel(order_ref, degree_ref, table_ref, field_ref, out_ref, low_pick, high_pick):
    pair = pl.program_id(0)
    rows = table_ref.shape[3]
    half = field_ref.shape[2] // 2

    @pl.when(pl.program_id(1) == 0)
    def _():
        low = order_ref[pair]
        degree = degree_ref[...]
        at = lax.broadcasted_iota(jnp.int32, low_pick.shape, 1)
        low_pick[...] = jnp.where(at == degree - low, 1.0, 0.0).astype(BF16)
        high = jnp.where(degree >= rows - 2 - low, degree + 1, -1)
        high_pick[...] = jnp.where(at == high, 1.0, 0.0).astype(BF16)

    coef = jnp.dot(field_ref[0, 0], table_ref[0, 0], preferred_element_type=F32).astype(BF16)
    low_rows = lax.dot_general(low_pick[...], coef[:half], LAST, preferred_element_type=F32)
    high_rows = lax.dot_general(high_pick[...], coef[half:], LAST, preferred_element_type=F32)
    dests, _, _, slots, _ = out_ref.shape
    out_ref[:, 0, 0, :, :half] = low_rows.reshape(dests, slots, half).astype(BF16)
    out_ref[:, 0, 0, :, half:] = high_rows.reshape(dests, slots, half).astype(BF16)


def synthesise_kernel(order_ref, degree_ref, table_ref, *refs):
    mixed_refs, (out_ref, low_pick, high_pick, held) = refs[:-4], refs[-4:]
    pair = pl.program_id(0)
    rows = table_ref.shape[3]
    half = held.shape[1] // 2

    @pl.when(pl.program_id(1) == 0)
    def _():
        low = order_ref[pair]
        degree = degree_ref[...]
        at = lax.broadcasted_iota(jnp.int32, low_pick.shape, 1)
        low_pick[...] = jnp.where(at == degree - low, 1.0, 0.0).astype(BF16)
        high = jnp.where(degree >= rows - 2 - low, degree + 1, -1)
        high_pick[...] = jnp.where(at == high, 1.0, 0.0).astype(BF16)

    for spin, mixed_ref in enumerate(mixed_refs):

        @pl.when(pl.program_id(1) == spin)
        def _(mixed_ref=mixed_ref):
            held[...] = mixed_ref[:, :, 0].astype(F32).reshape(held.shape).astype(BF16)

    mixed = held[...]
    low_rows = lax.dot_general(mixed[:, :half], low_pick[...], FIRST, preferred_element_type=F32)
    high_rows = lax.dot_general(mixed[:, half:], high_pick[...], FIRST, preferred_element_type=F32)
    back = jnp.concatenate([low_rows, high_rows], axis=0).astype(BF16)
    out_ref[0, 0] = lax.dot_general(
        back, table_ref[0, 0], LAST, preferred_element_type=F32
    ).astype(BF16)


def mix_kernel(slot_count, where_ref, x_ref, *refs):
    weights, out_ref = refs[:-1], refs[-1]
    blocks = len(weights)
    _, _, items, width = x_ref.shape
    chans = weights[0].shape[2]
    parts = width // chans
    me = where_ref[0]
    live = pl.program_id(0) < slot_count

    @pl.when(live)
    def _():
        held = []
        for shift in range(blocks):
            x = x_ref[0, lax.rem(me - shift + blocks, blocks)]
            held.append(
                jnp.concatenate([x[:, i * chans:(i + 1) * chans] for i in range(parts)], axis=0)
            )
        w = jnp.concatenate([weight[0, 0] for weight in weights], axis=0)
        y = jnp.dot(jnp.concatenate(held, axis=1), w, preferred_element_type=F32).astype(BF16)
        for g in range(blocks):
            out_ref[0, lax.rem(g - me + blocks, blocks)] = jnp.concatenate(
                [y[i * items:(i + 1) * items, g * chans:(g + 1) * chans] for i in range(parts)],
                axis=1,
            )

    @pl.when(jnp.logical_not(live))
    def _():
        out_ref[...] = jnp.zeros_like(out_ref)


def per_device(fields, wigner, mix_weight, pair_orders, deg_counts):
    pairs, spins, cycles, _, _, chans = fields.shape
    rows = wigner.shape[2]
    width = 4 * chans
    owners, blocks = lax.axis_size("order"), lax.axis_size("chan")
    slots = mix_weight.shape[0] // blocks
    padded = -(-slots // 8) * 8
    dests = owners * blocks
    me = lax.axis_index("chan")

    starts = jnp.cumsum(deg_counts) - deg_counts
    within = jnp.arange(padded, dtype=jnp.int32)
    slot = jnp.arange(blocks, dtype=jnp.int32)[:, None] * slots + within[None, :]
    real = (within[None, None, :] < slots) & (slot[None] < deg_counts[:, None, None])
    degree = jnp.where(real, starts[:, None, None] + slot[None], -(1 << 20))
    sources = lax.rem(me - jnp.arange(blocks, dtype=jnp.int32) + blocks, blocks)
    degree_back = jnp.take(degree, sources, axis=1).reshape(-1, 1)
    degree = degree.reshape(-1, 1)
    total = dests * padded

    rings = [[(g, (g + d) % blocks) for g in range(blocks)] for d in range(1, blocks)]
    rings = [[(g, (g + d) % blocks) for g in range(blocks)] for d in range(1, blocks)]
    sent = []
    for shift in range(1, blocks):
        to = lax.rem(me + shift, blocks)
        sent.append(lax.dynamic_slice_in_dim(mix_weight, to * slots, slots, axis=0))
    degree, *sent = lax.optimization_barrier((degree, *sent))
    arrived = [lax.ppermute(sent[d], "chan", rings[d]) for d in range(blocks - 1)]
    table = wigner.transpose(0, 1, 3, 2)
    lines = fields.transpose(0, 1, 3, 4, 5, 2).reshape(pairs, spins, width, cycles)

    table_spec = pl.BlockSpec((1, 1, cycles, rows), lambda p, s, o: (p, s, 0, 0))
    field_spec = pl.BlockSpec((1, 1, width, cycles), lambda p, s, o: (p, s, 0, 0))
    moved_spec = pl.BlockSpec((dests, 1, 1, padded, width), lambda p, s, o: (0, p, s, 0, 0))
    moved = jax.ShapeDtypeStruct((dests, pairs, spins, padded, width), BF16)
    table_flops = 4 * pairs * spins * rows * cycles * width
    cost = pl.CostEstimate(flops=table_flops, bytes_accessed=2 * wigner.size * 2, transcendentals=0)

    outgoing = pl.pallas_call(
        analyse_kernel,
        out_shape=moved,
        grid_spec=pltpu.PrefetchScalarGridSpec(
            num_scalar_prefetch=1,
            grid=(pairs, spins),
            in_specs=[pl.BlockSpec((total, 1), lambda p, s, o: (0, 0)), table_spec, field_spec],
            out_specs=moved_spec,
            scratch_shapes=[pltpu.VMEM((total, rows), BF16)] * 2,
        ),
        compiler_params=PARAMS,
        cost_estimate=cost,
        name="analyse",
    )(pair_orders, degree, table, lines)

    received = lax.all_to_all(outgoing, ("order", "chan"), split_axis=0, concat_axis=0, tiled=True)
    received = received.reshape(owners, blocks, pairs, spins, padded, width)
    items = owners * pairs
    x_shape = (padded, blocks, items, width)

    def block_at(k):
        return jnp.minimum(k, slots - 1)

    crossings, returned = [], []
    for spin in range(spins):
        x = received[:, :, :, spin].transpose(3, 1, 0, 2, 4).reshape(x_shape)
        block = (1, 1, chans, mix_weight.shape[3])
        specs = [
            pl.BlockSpec(block, lambda k, w, spin=spin: (w[0] * slots + block_at(k), spin, 0, 0))
        ]
        specs += [
            pl.BlockSpec(block, lambda k, w, spin=spin: (block_at(k), spin, 0, 0))
        ] * (blocks - 1)
        x_spec = pl.BlockSpec((1,) + x_shape[1:], lambda k, w: (k, 0, 0, 0))
        mixed = pl.pallas_call(
            functools.partial(mix_kernel, slots),
            out_shape=jax.ShapeDtypeStruct(x_shape, BF16),
            grid_spec=pltpu.PrefetchScalarGridSpec(
                num_scalar_prefetch=1, grid=(padded,), in_specs=[x_spec] + specs, out_specs=x_spec
            ),
            compiler_params=PARAMS,
            cost_estimate=pl.CostEstimate(
                flops=2 * padded * 4 * items * (blocks * chans) ** 2,
                bytes_accessed=4 * padded * blocks * items * width,
                transcendentals=0,
            ),
            name="mix",
        )(me.reshape(1).astype(jnp.int32), x, mix_weight, *arrived)
        mixed = mixed.reshape(padded, blocks, owners, pairs, width).transpose(1, 2, 3, 0, 4)
        crossed = [mixed[0]]
        for shift in range(1, blocks):
            crossed.append(lax.ppermute(mixed[shift], "chan", rings[shift - 1]))
        crossings.append(crossed)
    for spin in range(spins):
        crossed = crossings[spin]
        if spin + 1 < spins:
            later = crossings[spin + 1]
            *crossed, later[0] = lax.optimization_barrier((*crossed, later[0]))
        crossed = jnp.stack(crossed, axis=1)
        returned.append(lax.all_to_all(crossed, "order", split_axis=0, concat_axis=0, tiled=True))

    back_spec = pl.BlockSpec((owners, blocks, 1, padded, width), lambda p, s, o: (0, 0, p, 0, 0))
    out = pl.pallas_call(
        synthesise_kernel,
        out_shape=jax.ShapeDtypeStruct((pairs, spins, width, cycles), BF16),
        grid_spec=pltpu.PrefetchScalarGridSpec(
            num_scalar_prefetch=1,
            grid=(pairs, spins),
            in_specs=[pl.BlockSpec((total, 1), lambda p, s, o: (0, 0)), table_spec]
            + [back_spec] * spins,
            out_specs=field_spec,
            scratch_shapes=[pltpu.VMEM((total, rows), BF16)] * 2
            + [pltpu.VMEM((total, width), BF16)],
        ),
        compiler_params=PARAMS,
        cost_estimate=cost,
        name="synthesise",
    )(pair_orders, degree_back, table, *returned)
    return out.reshape(pairs, spins, 2, 2, chans, cycles).transpose(0, 1, 5, 2, 3, 4)


def solution(mesh):
    in_specs = (
        P("order", None, None, None, None, "chan"),
        P("order", None, None, None),
        P("order", None, "chan", None),
        P("order"),
        P(),
    )
    out_specs = P("order", None, None, None, None, "chan")
    return jax.shard_map(
        per_device, mesh=mesh, in_specs=in_specs, out_specs=out_specs, check_vma=False
    )
```

```python
import functools
import jax
import jax.numpy as jnp
from jax import lax
from jax.experimental import pallas as pl
from jax.experimental.pallas import tpu as pltpu
from jax.sharding import PartitionSpec as P

F32, BF16 = jnp.float32, jnp.bfloat16
FIRST = (((0,), (0,)), ((), ()))
LAST = (((1,), (1,)), ((), ()))
PARAMS = pltpu.CompilerParams(vmem_limit_bytes=48 * 1024 * 1024)


def analyse_kernel(order_ref, degree_ref, table_ref, field_ref, out_ref, low_pick, high_pick):
    pair = pl.program_id(0)
    rows = table_ref.shape[3]
    half = field_ref.shape[2] // 2

    @pl.when(pl.program_id(1) == 0)
    def _():
        low = order_ref[pair]
        degree = degree_ref[...]
        at = lax.broadcasted_iota(jnp.int32, low_pick.shape, 1)
        low_pick[...] = jnp.where(at == degree - low, 1.0, 0.0).astype(BF16)
        high = jnp.where(degree >= rows - 2 - low, degree + 1, -1)
        high_pick[...] = jnp.where(at == high, 1.0, 0.0).astype(BF16)

    coef = jnp.dot(field_ref[0, 0], table_ref[0, 0], preferred_element_type=F32).astype(BF16)
    low_rows = lax.dot_general(low_pick[...], coef[:half], LAST, preferred_element_type=F32)
    high_rows = lax.dot_general(high_pick[...], coef[half:], LAST, preferred_element_type=F32)
    dests, _, _, slots, _ = out_ref.shape
    out_ref[:, 0, 0, :, :half] = low_rows.reshape(dests, slots, half).astype(BF16)
    out_ref[:, 0, 0, :, half:] = high_rows.reshape(dests, slots, half).astype(BF16)


def synthesise_kernel(order_ref, degree_ref, table_ref, mixed_ref, out_ref, low_pick, high_pick):
    pair = pl.program_id(0)
    rows = table_ref.shape[3]
    half = mixed_ref.shape[4] // 2

    @pl.when(pl.program_id(1) == 0)
    def _():
        low = order_ref[pair]
        degree = degree_ref[...]
        at = lax.broadcasted_iota(jnp.int32, low_pick.shape, 1)
        low_pick[...] = jnp.where(at == degree - low, 1.0, 0.0).astype(BF16)
        high = jnp.where(degree >= rows - 2 - low, degree + 1, -1)
        high_pick[...] = jnp.where(at == high, 1.0, 0.0).astype(BF16)

    dests, _, _, slots, width = mixed_ref.shape
    mixed = mixed_ref[:, 0, 0].astype(F32).reshape(dests * slots, width).astype(BF16)
    low_rows = lax.dot_general(mixed[:, :half], low_pick[...], FIRST, preferred_element_type=F32)
    high_rows = lax.dot_general(mixed[:, half:], high_pick[...], FIRST, preferred_element_type=F32)
    back = jnp.concatenate([low_rows, high_rows], axis=0).astype(BF16)
    out_ref[0, 0] = lax.dot_general(
        back, table_ref[0, 0], LAST, preferred_element_type=F32
    ).astype(BF16)


def mix_kernel(slot_count, where_ref, x_ref, *refs):
    weights, out_ref = refs[:-1], refs[-1]
    blocks = len(weights)
    _, spins, _, items, width = x_ref.shape
    chans = weights[0].shape[2]
    parts = width // chans
    me = where_ref[0]
    live = pl.program_id(0) < slot_count

    @pl.when(live)
    def _():
        for s in range(spins):
            held = []
            for shift in range(blocks):
                x = x_ref[0, s, lax.rem(me - shift + blocks, blocks)]
                held.append(
                    jnp.concatenate([x[:, i * chans:(i + 1) * chans] for i in range(parts)], axis=0)
                )
            w = jnp.concatenate([weight[0, s] for weight in weights], axis=0)
            y = jnp.dot(jnp.concatenate(held, axis=1), w, preferred_element_type=F32).astype(BF16)
            for g in range(blocks):
                out_ref[0, s, g] = jnp.concatenate(
                    [y[i * items:(i + 1) * items, g * chans:(g + 1) * chans] for i in range(parts)],
                    axis=1,
                )

    @pl.when(jnp.logical_not(live))
    def _():
        out_ref[...] = jnp.zeros_like(out_ref)


def per_device(fields, wigner, mix_weight, pair_orders, deg_counts):
    pairs, spins, cycles, _, _, chans = fields.shape
    rows = wigner.shape[2]
    width = 4 * chans
    owners, blocks = lax.axis_size("order"), lax.axis_size("chan")
    slots = mix_weight.shape[0] // blocks
    padded = -(-slots // 8) * 8
    dests = owners * blocks
    me = lax.axis_index("chan")

    starts = jnp.cumsum(deg_counts) - deg_counts
    within = jnp.arange(padded, dtype=jnp.int32)
    slot = jnp.arange(blocks, dtype=jnp.int32)[:, None] * slots + within[None, :]
    real = (within[None, None, :] < slots) & (slot[None] < deg_counts[:, None, None])
    degree = jnp.where(real, starts[:, None, None] + slot[None], -(1 << 20)).reshape(-1, 1)
    total = dests * padded

    sent = []
    for shift in range(1, blocks):
        to = lax.rem(me + shift, blocks)
        sent.append(lax.dynamic_slice_in_dim(mix_weight, to * slots, slots, axis=0))
    degree, *sent = lax.optimization_barrier((degree, *sent))
    weights = [mix_weight]
    for shift in range(1, blocks):
        ring = [(g, (g + shift) % blocks) for g in range(blocks)]
        weights.append(lax.ppermute(sent[shift - 1], "chan", ring))
    table = wigner.transpose(0, 1, 3, 2)
    lines = fields.transpose(0, 1, 3, 4, 5, 2).reshape(pairs, spins, width, cycles)

    table_spec = pl.BlockSpec((1, 1, cycles, rows), lambda p, s, o: (p, s, 0, 0))
    field_spec = pl.BlockSpec((1, 1, width, cycles), lambda p, s, o: (p, s, 0, 0))
    moved_spec = pl.BlockSpec((dests, 1, 1, padded, width), lambda p, s, o: (0, p, s, 0, 0))
    moved = jax.ShapeDtypeStruct((dests, pairs, spins, padded, width), BF16)
    table_flops = 4 * pairs * spins * rows * cycles * width
    cost = pl.CostEstimate(flops=table_flops, bytes_accessed=2 * wigner.size * 2, transcendentals=0)

    outgoing = pl.pallas_call(
        analyse_kernel,
        out_shape=moved,
        grid_spec=pltpu.PrefetchScalarGridSpec(
            num_scalar_prefetch=1,
            grid=(pairs, spins),
            in_specs=[pl.BlockSpec((total, 1), lambda p, s, o: (0, 0)), table_spec, field_spec],
            out_specs=moved_spec,
            scratch_shapes=[pltpu.VMEM((total, rows), BF16)] * 2,
        ),
        compiler_params=PARAMS,
        cost_estimate=cost,
        name="analyse",
    )(pair_orders, degree, table, lines)

    received = lax.all_to_all(outgoing, ("order", "chan"), split_axis=0, concat_axis=0, tiled=True)
    received = received.reshape(owners, blocks, pairs, spins, padded, width)
    items = owners * pairs
    x = received.transpose(4, 3, 1, 2, 0, 5).reshape(padded, spins, blocks, items, width)

    def block_at(k):
        return jnp.minimum(k, slots - 1)

    weight_block = (1, spins, chans, mix_weight.shape[3])
    weight_specs = [pl.BlockSpec(weight_block, lambda k, w: (w[0] * slots + block_at(k), 0, 0, 0))]
    weight_specs += [pl.BlockSpec(weight_block, lambda k, w: (block_at(k), 0, 0, 0))] * (blocks - 1)
    x_spec = pl.BlockSpec((1, spins, blocks, items, width), lambda k, w: (k, 0, 0, 0, 0))
    mixed = pl.pallas_call(
        functools.partial(mix_kernel, slots),
        out_shape=jax.ShapeDtypeStruct(x.shape, BF16),
        grid_spec=pltpu.PrefetchScalarGridSpec(
            num_scalar_prefetch=1,
            grid=(padded,),
            in_specs=[x_spec] + weight_specs,
            out_specs=x_spec,
        ),
        compiler_params=PARAMS,
        name="mix",
    )(me.reshape(1).astype(jnp.int32), x, *weights)

    mixed = mixed.reshape(padded, spins, blocks, pairs, owners, width).transpose(4, 2, 3, 1, 0, 5)
    mixed = mixed.reshape(dests, pairs, spins, padded, width)
    returned = lax.all_to_all(mixed, ("order", "chan"), split_axis=0, concat_axis=0, tiled=True)

    out = pl.pallas_call(
        synthesise_kernel,
        out_shape=jax.ShapeDtypeStruct((pairs, spins, width, cycles), BF16),
        grid_spec=pltpu.PrefetchScalarGridSpec(
            num_scalar_prefetch=1,
            grid=(pairs, spins),
            in_specs=[pl.BlockSpec((total, 1), lambda p, s, o: (0, 0)), table_spec, moved_spec],
            out_specs=field_spec,
            scratch_shapes=[pltpu.VMEM((total, rows), BF16)] * 2,
        ),
        compiler_params=PARAMS,
        cost_estimate=cost,
        name="synthesise",
    )(pair_orders, degree, table, returned)
    return out.reshape(pairs, spins, 2, 2, chans, cycles).transpose(0, 1, 5, 2, 3, 4)


def solution(mesh):
    in_specs = (
        P("order", None, None, None, None, "chan"),
        P("order", None, None, None),
        P("order", None, "chan", None),
        P("order"),
        P(),
    )
    out_specs = P("order", None, None, None, None, "chan")
    return jax.shard_map(
        per_device, mesh=mesh, in_specs=in_specs, out_specs=out_specs, check_vma=False
    )
```
